256 devices in a mesh: wide: 32 (over z, y), narrow: 8 (over x, core).
Axes of the slice: x: 4, y: 4, z: 8, core: 2. Of those that a mesh axis runs over, the one named last changes fastest.
Arguments:
- snapshots: float32 [1048576, 512], P(('wide', 'narrow')), may hold values from -300 to 300
- test_matrix: float32 [512, 128], replicated, may hold values from -0.25 to 0.25
Outputs:
- basis: float32 [1048576, 128], P(('wide', 'narrow'))
- coefficients: float32 [128, 512], replicated
The draws below stay inside these ranges and needn't reach their ends.
All inputs are finite; a program needn't handle non-finite values.
Results may differ from the reference program's by a relative error of at most 0.000092.
Values sent between devices are 32-bit elements; how exact they have to be, the bound alone decides.
A program may use at most 64 MiB of HBM per device.

```python
import math
import jax
import jax.numpy as jnp
from jax import lax

SNAPS = 512
RANK = 128
ROWS = 1048576


def draw_snapshots(key, part):
    key = jax.random.fold_in(key, 11)
    keys = jax.random.split(key, 3)
    base = jax.random.truncated_normal(keys[0], -4.0, 4.0, (ROWS, SNAPS), jnp.float32)
    colscale = jnp.exp(jax.random.uniform(keys[1], (1, SNAPS), jnp.float32, 0.0, math.log(10.0)))
    ramp = 1.0 + 2.0 * jnp.arange(ROWS, dtype=jnp.float32)[:, None] / ROWS
    rowscale = ramp * jnp.exp(jax.random.uniform(keys[2], (ROWS, 1), jnp.float32, -0.5, 0.5))
    values = base * colscale * rowscale
    return values


def gaussian(own_key, dims, deviation, reach, held_as=jnp.bfloat16):
    array = deviation * jax.random.normal(own_key, dims, jnp.float32)
    return jnp.clip(array, min=-reach, max=reach).astype(held_as)


def setup_inputs(seed: int = 0) -> dict:
    arg_keys = jax.random.split(jax.random.key(seed), 3)
    snapshots = draw_snapshots(jax.random.fold_in(arg_keys[2], 71), 0)
    test_matrix = gaussian(arg_keys[1], (SNAPS, RANK), SNAPS ** -0.5, 0.25, jnp.float32)
    return {"snapshots": snapshots, "test_matrix": test_matrix}


def reference(snapshots, test_matrix):
    hi = lax.Precision.HIGHEST
    sketch = jnp.dot(snapshots.astype(jnp.float32), test_matrix.astype(jnp.float32), precision=hi, preferred_element_type=jnp.float32)
    gram = jnp.dot(sketch.T.astype(jnp.float32), sketch.astype(jnp.float32), precision=hi, preferred_element_type=jnp.float32)
    lower = jnp.linalg.cholesky(gram)
    inverse = lax.linalg.triangular_solve(lower, jnp.eye(RANK, dtype=jnp.float32), left_side=True, lower=True)
    ortho = jnp.dot(sketch.astype(jnp.float32), inverse.T.astype(jnp.float32), precision=hi, preferred_element_type=jnp.float32)
    scale = jnp.sqrt(jnp.float32(ROWS))
    coefficients = jnp.dot(ortho.T.astype(jnp.float32), snapshots.astype(jnp.float32), precision=hi, preferred_element_type=jnp.float32) / scale
    return (ortho * scale, coefficients)
```

```python
import functools

import jax
import jax.numpy as jnp
from jax import lax
from jax.experimental import pallas as pl
from jax.experimental.pallas import tpu as pltpu
from jax.sharding import PartitionSpec as P

MESH = pl.DeviceIdType.MESH
ROW = 4
CHUNKS = 8
F32 = jnp.float32
BF16 = jnp.bfloat16


def halves(x):
    high = x.astype(BF16)
    return high, (x - high.astype(F32)).astype(BF16)


def dot(a, b, dims=((1,), (0,))):
    return lax.dot_general(a, b, (dims, ((), ())), preferred_element_type=F32)


def reduce_kernel(
    plane, depth, lines,
    a_hbm, omega_ref, s_hbm, g_ref, p_ref,
    a, s, xt, ah, al, gram, proj,
    g_mine, g_in, g_z, g_all, p_mine, p_in, p_z, p_all,
    load_sem, store_sem, g_send, g_recv, p_send, p_recv,
):
    wide, narrow = lax.axis_index("wide"), lax.axis_index("narrow")
    z, y = wide // ROW, wide % ROW
    me = y * lines + narrow

    def in_plane(d):
        t = lax.rem(me + d, plane)
        return t, (z * ROW + t // lines, lax.rem(t, lines))

    def along_z(d):
        t = lax.rem(z + d, depth)
        return t, (t * ROW + y, narrow)

    rows = a.shape[0] // CHUNKS

    def load(c):
        part = pl.ds(c * rows, rows)
        return pltpu.make_async_copy(a_hbm.at[part], a.at[part], load_sem.at[c])

    for c in range(CHUNKS):
        load(c).start()

    barrier = pltpu.get_barrier_semaphore()

    @pl.loop(1, plane)
    def _(d):
        pl.semaphore_signal(barrier, inc=1, device_id=in_plane(d)[1], device_id_type=MESH)

    @pl.loop(1, depth)
    def _(d):
        pl.semaphore_signal(barrier, inc=1, device_id=along_z(d)[1], device_id_type=MESH)

    def send(src, dst, where, sems, phase):
        pltpu.make_async_remote_copy(
            src_ref=src, dst_ref=dst, send_sem=sems[0].at[phase], recv_sem=sems[1].at[phase],
            device_id=where, device_id_type=MESH,
        ).start()

    def settle(ref, sem):
        pltpu.make_async_copy(ref, ref, sem).wait()

    def scatter(mine, into, sems):
        @pl.loop(1, plane)
        def _(d):
            t, where = in_plane(d)
            send(mine.at[t], into.at[d - 1], where, sems, 0)

    def across(mine, into, slots, sems):
        settle(into, sems[1].at[0])
        slots[z] = mine[me] + jnp.sum(into[...], axis=0)

        @pl.loop(1, depth)
        def _(d):
            send(slots.at[z], slots.at[z], along_z(d)[1], sems, 1)

    def gather(slots, whole, sems):
        settle(slots.at[pl.ds(0, depth - 1)], sems[1].at[1])
        whole[me] = jnp.sum(slots[...], axis=0)

        @pl.loop(1, plane)
        def _(d):
            send(whole.at[me], whole.at[me], in_plane(d)[1], sems, 2)

    def arrived(whole, sems):
        settle(whole.at[pl.ds(0, plane - 1)], sems[1].at[2])

    def sent(mine, slots, sems):
        settle(mine.at[pl.ds(0, plane - 1)], sems[0].at[0])
        settle(slots.at[pl.ds(0, depth - 1)], sems[0].at[1])
        settle(mine.at[pl.ds(0, plane - 1)], sems[0].at[2])

    rank = omega_ref.shape[1]
    oh, ol = halves(omega_ref[...])
    both = jnp.concatenate([oh, ol], axis=1)
    gram[...] = jnp.zeros_like(gram)
    proj[...] = jnp.zeros_like(proj)

    @pl.loop(0, CHUNKS)
    def _(c):
        load(c).wait()
        part = pl.ds(pl.multiple_of(c * rows, rows), rows)
        high, low = halves(a[part, :])
        ah[part, :] = high
        al[part, :] = low
        wide_s = dot(high, both)
        s_c = wide_s[:, :rank] + wide_s[:, rank:] + dot(low, oh)
        s[part, :] = s_c
        x = jnp.concatenate(halves(s_c), axis=1)
        x_t = x.T
        xt[:, part] = x_t
        gram[...] += dot(x_t, x)

    save = pltpu.make_async_copy(s, s_hbm, store_sem)
    save.start()
    g = gram[...]
    g_mine[...] = (g[:rank, :rank] + g[:rank, rank:] + g[rank:, :rank] + g[rank:, rank:]).reshape(g_mine.shape)
    pl.semaphore_wait(barrier, plane + depth - 2)
    g_sems, p_sems = (g_send, g_recv), (p_send, p_recv)
    scatter(g_mine, g_in, g_sems)

    def project(first, last):
        @pl.loop(first, last)
        def _(c):
            part = pl.ds(pl.multiple_of(c * rows, rows), rows)
            x_t = xt[:, part]
            w = dot(x_t, ah[part, :])
            proj[...] += w[:rank] + w[rank:] + dot(x_t[:rank], al[part, :])

    project(0, CHUNKS // 2)
    across(g_mine, g_in, g_z, g_sems)
    project(CHUNKS // 2, CHUNKS)
    tall = p_mine.shape[1]
    per = rank // tall
    for b in range(p_mine.shape[0] // per):
        p_mine[b * per:(b + 1) * per] = proj[:, b * 128:(b + 1) * 128].reshape(per, tall, 128)
    gather(g_z, g_all, g_sems)
    scatter(p_mine, p_in, p_sems)
    arrived(g_all, g_sems)
    g_ref[...] = g_all[...].reshape(g_ref.shape)
    across(p_mine, p_in, p_z, p_sems)
    gather(p_z, p_all, p_sems)
    sent(g_mine, g_z, g_sems)
    save.wait()
    arrived(p_all, p_sems)
    for b in range(p_mine.shape[0] // per):
        p_ref[:, b * 128:(b + 1) * 128] = p_all[b * per:(b + 1) * per].reshape(rank, 128)
    sent(p_mine, p_z, p_sems)


def reduced(plane, depth, lines, snapshots, test_matrix):
    rows, snaps = snapshots.shape
    rank = test_matrix.shape[1]
    g_piece = (rank // plane, rank)
    p_piece = (rank * snaps // 128 // plane, 128)
    vmem = pl.BlockSpec(memory_space=pltpu.VMEM)
    hbm = pl.BlockSpec(memory_space=pltpu.HBM)

    def exchange(piece):
        return [pltpu.VMEM((n,) + piece, F32) for n in (plane, plane - 1, depth, plane)]

    return pl.pallas_call(
        functools.partial(reduce_kernel, plane, depth, lines),
        out_shape=(
            jax.ShapeDtypeStruct((rows, rank), F32),
            jax.ShapeDtypeStruct((rank, rank), F32),
            jax.ShapeDtypeStruct((rank, snaps), F32),
        ),
        in_specs=[hbm, vmem],
        out_specs=(hbm, vmem, vmem),
        scratch_shapes=[
            pltpu.VMEM((rows, snaps), F32),
            pltpu.VMEM((rows, rank), F32),
            pltpu.VMEM((2 * rank, rows), BF16),
            pltpu.VMEM((rows, snaps), BF16),
            pltpu.VMEM((rows, snaps), BF16),
            pltpu.VMEM((2 * rank, 2 * rank), F32),
            pltpu.VMEM((rank, snaps), F32),
            *exchange(g_piece),
            *exchange(p_piece),
            pltpu.SemaphoreType.DMA((CHUNKS,)),
            pltpu.SemaphoreType.DMA,
            pltpu.SemaphoreType.DMA((3,)),
            pltpu.SemaphoreType.DMA((3,)),
            pltpu.SemaphoreType.DMA((3,)),
            pltpu.SemaphoreType.DMA((3,)),
        ],
        compiler_params=pltpu.CompilerParams(
            collective_id=0, has_side_effects=True, vmem_limit_bytes=48 << 20
        ),
        name="reduced",
    )(snapshots, test_matrix)


def on_device(plane, depth, lines, snapshots, test_matrix):
    hi = lax.Precision.HIGHEST
    rank = test_matrix.shape[1]
    total_rows = snapshots.shape[0] * plane * depth
    scale = jnp.sqrt(F32(total_rows))
    sketch, gram, proj = reduced(plane, depth, lines, snapshots, test_matrix)
    lower = jnp.linalg.cholesky(gram)
    inverse = lax.linalg.triangular_solve(lower, jnp.eye(rank, dtype=F32), left_side=True, lower=True)
    basis = jnp.dot(sketch, inverse.T * scale, precision=hi, preferred_element_type=F32)
    coefficients = jnp.dot(inverse, proj, precision=hi, preferred_element_type=F32) / scale
    return basis, coefficients


def solution(mesh):
    wide, lines = mesh.shape["wide"], mesh.shape["narrow"]
    plane, depth = ROW * lines, wide // ROW
    return jax.shard_map(
        functools.partial(on_device, plane, depth, lines),
        mesh=mesh,
        in_specs=(P(("wide", "narrow"), None), P()),
        out_specs=(P(("wide", "narrow"), None), P()),
        check_vma=False,
    )
```

```python
import functools
import math

import jax
import jax.numpy as jnp
from jax import lax
from jax.experimental import pallas as pl
from jax.experimental.pallas import tpu as pltpu
from jax.sharding import PartitionSpec as P

MESH = pl.DeviceIdType.MESH
ROW = 4
CHUNKS = 8
PANEL = 8
TURN = 3
F32 = jnp.float32
BF16 = jnp.bfloat16


def halves(x):
    high = x.astype(BF16)
    return high, (x - high.astype(F32)).astype(BF16)


def dot(a, b, dims=((1,), (0,))):
    return lax.dot_general(a, b, (dims, ((), ())), preferred_element_type=F32)


def inverse_factor(g):
    n = g.shape[0]
    row = lax.broadcasted_iota(jnp.int32, (n, n), 0)
    col = lax.broadcasted_iota(jnp.int32, (n, n), 1)
    w = jnp.where(row == col, F32(1), F32(0))
    at = lax.broadcasted_iota(jnp.int32, (PANEL, n), 0)
    for first in range(0, n, PANEL):
        columns = [jnp.broadcast_to(g[:, first + k:first + k + 1], g.shape) for k in range(PANEL)]
        top = [c[:PANEL] for c in columns]
        rest = [c[PANEL:] for c in columns]
        g_top, w_top = g[:PANEL], w[:PANEL]
        steps = []
        panel = jnp.zeros((PANEL, n), F32)
        for i in range(PANEL):
            r = lax.rsqrt(top[i][i:i + 1])
            u, v = g_top[i:i + 1] * r, w_top[i:i + 1] * r
            m = top[i] * r
            ahead = {}
            for k in range(i + 1, PANEL):
                ahead[k] = top[k][i:i + 1] * r
                top[k] = top[k] - m * ahead[k]
            if i + 1 < PANEL:
                g_top, w_top = g_top - m * u, w_top - m * v
            panel = jnp.where(at == i, v, panel)
            steps.append((r, u, v, ahead))
        if first + PANEL < n:
            g, w = g[PANEL:], w[PANEL:]
            for i, (r, u, v, ahead) in enumerate(steps):
                m = rest[i] * r
                for k in ahead:
                    rest[k] = rest[k] - m * ahead[k]
                g, w = g - m * u, w - m * v
        yield panel


def reduce_kernel(
    plane, depth, lines,
    a_hbm, omega_hbm, basis_hbm, coef_ref,
    a, omega, s, xt, ah, al, gram, proj,
    g_mine, g_in, g_z, g_all, p_mine, p_in, p_z, p_all,
    load_sem, store_sem, g_send, g_recv, p_send, p_recv,
):
    wide, narrow = lax.axis_index("wide"), lax.axis_index("narrow")
    z, y = wide // ROW, wide % ROW
    me = y * lines + narrow

    def in_plane(d):
        t = lax.rem(me + d, plane)
        return t, (z * ROW + t // lines, lax.rem(t, lines))

    def along_z(d):
        t = lax.rem(z + d, depth)
        return t, (t * ROW + y, narrow)

    rows = a.shape[0] // CHUNKS

    def load(c):
        part = pl.ds(c * rows, rows)
        return pltpu.make_async_copy(a_hbm.at[part], a.at[part], load_sem.at[c])

    load_omega = pltpu.make_async_copy(omega_hbm, omega, load_sem.at[CHUNKS])
    load_omega.start()
    for c in range(CHUNKS):
        load(c).start()

    barrier = pltpu.get_barrier_semaphore()

    @pl.loop(1, plane)
    def _(d):
        pl.semaphore_signal(barrier, inc=1, device_id=in_plane(d)[1], device_id_type=MESH)

    @pl.loop(1, depth)
    def _(d):
        pl.semaphore_signal(barrier, inc=1, device_id=along_z(d)[1], device_id_type=MESH)

    def send(src, dst, where, sems, phase):
        pltpu.make_async_remote_copy(
            src_ref=src, dst_ref=dst, send_sem=sems[0].at[phase], recv_sem=sems[1].at[phase],
            device_id=where, device_id_type=MESH,
        ).start()

    def settle(ref, sem):
        pltpu.make_async_copy(ref, ref, sem).wait()

    def scatter(mine, into, sems):
        @pl.loop(1, plane)
        def _(d):
            t, where = in_plane(d)
            send(mine.at[t], into.at[d - 1], where, sems, 0)

    def across(mine, into, slots, sems):
        settle(into, sems[1].at[0])
        slots[z] = mine[me] + jnp.sum(into[...], axis=0)

        @pl.loop(1, depth)
        def _(d):
            send(slots.at[z], slots.at[z], along_z(d)[1], sems, 1)

    def gather(slots, whole, sems):
        settle(slots.at[pl.ds(0, depth - 1)], sems[1].at[1])
        whole[me] = jnp.sum(slots[...], axis=0)

        @pl.loop(1, plane)
        def _(d):
            send(whole.at[me], whole.at[me], in_plane(d)[1], sems, 2)

    def arrived(whole, sems):
        settle(whole.at[pl.ds(0, plane - 1)], sems[1].at[2])

    def sent(mine, slots, sems):
        settle(mine.at[pl.ds(0, plane - 1)], sems[0].at[0])
        settle(slots.at[pl.ds(0, depth - 1)], sems[0].at[1])
        settle(mine.at[pl.ds(0, plane - 1)], sems[0].at[2])

    rank = omega.shape[1]
    load_omega.wait()
    oh, ol = halves(omega[...])
    both = jnp.concatenate([oh, ol], axis=1)
    gram[...] = jnp.zeros_like(gram)
    proj[...] = jnp.zeros_like(proj)

    @pl.loop(0, CHUNKS)
    def _(c):
        load(c).wait()
        part = pl.ds(pl.multiple_of(c * rows, rows), rows)
        high, low = halves(a[part, :])
        ah[part, :] = high
        al[part, :] = low
        wide_s = dot(high, both)
        s_c = wide_s[:, :rank] + wide_s[:, rank:] + dot(low, oh)
        s[part, :] = s_c
        x = jnp.concatenate(halves(s_c), axis=1)
        x_t = x.T
        xt[:, part] = x_t
        gram[...] += dot(x_t, x)

    g = gram[...]
    g_mine[...] = (g[:rank, :rank] + g[:rank, rank:] + g[rank:, :rank] + g[rank:, rank:]).reshape(g_mine.shape)
    pl.semaphore_wait(barrier, plane + depth - 2)
    g_sems, p_sems = (g_send, g_recv), (p_send, p_recv)
    scatter(g_mine, g_in, g_sems)

    def project(first, last):
        @pl.loop(first, last)
        def _(c):
            part = pl.ds(pl.multiple_of(c * rows, rows), rows)
            x_t = xt[:, part]
            w = dot(x_t, ah[part, :])
            proj[...] += w[:rank] + w[rank:] + dot(x_t[:rank], al[part, :])

    project(0, CHUNKS)
    tall = p_mine.shape[1]
    per = rank // tall
    for b in range(p_mine.shape[0] // per):
        p_mine[b * per:(b + 1) * per] = proj[:, b * 128:(b + 1) * 128].reshape(per, tall, 128)
    scatter(p_mine, p_in, p_sems)
    across(g_mine, g_in, g_z, g_sems)
    gather(g_z, g_all, g_sems)
    across(p_mine, p_in, p_z, p_sems)
    arrived(g_all, g_sems)

    panels = []
    for panel in inverse_factor(g_all[...].reshape(rank, rank)):
        panels.append(panel)
        if len(panels) == TURN:
            gather(p_z, p_all, p_sems)
    inverse = jnp.concatenate(panels, axis=0)
    scale = math.sqrt(a.shape[0] * plane * depth)
    wh, wl = halves(inverse * scale)
    both_w = jnp.concatenate([jnp.concatenate([wh, wh], axis=1), jnp.concatenate([wl, wl], axis=1)], axis=0)

    def store(c):
        part = pl.ds(c * rows, rows)
        return pltpu.make_async_copy(s.at[part], basis_hbm.at[part], store_sem.at[c])

    @pl.loop(0, CHUNKS)
    def _(c):
        part = pl.ds(pl.multiple_of(c * rows, rows), rows)
        x = jnp.concatenate(halves(s[part, :]), axis=1)
        wide_b = dot(x, both_w, ((1,), (1,)))
        s[part, :] = wide_b[:, :rank] + wide_b[:, rank:]
        store(c).start()

    sent(g_mine, g_z, g_sems)
    arrived(p_all, p_sems)
    ch, cl = halves(inverse * (1.0 / scale))
    left = jnp.concatenate([ch, cl, ch, cl], axis=1)
    for b in range(p_mine.shape[0] // per):
        ph, p_low = halves(p_all[b * per:(b + 1) * per].reshape(rank, 128))
        right = jnp.concatenate([ph, ph, p_low, p_low], axis=0)
        coef_ref[:, b * 128:(b + 1) * 128] = dot(left, right)
    sent(p_mine, p_z, p_sems)

    @pl.loop(0, CHUNKS)
    def _(c):
        store(c).wait()


def reduced(plane, depth, lines, snapshots, test_matrix):
    rows, snaps = snapshots.shape
    rank = test_matrix.shape[1]
    g_piece = (rank // plane, rank)
    p_piece = (rank * snaps // 128 // plane, 128)
    vmem = pl.BlockSpec(memory_space=pltpu.VMEM)
    hbm = pl.BlockSpec(memory_space=pltpu.HBM)

    def exchange(piece):
        return [pltpu.VMEM((n,) + piece, F32) for n in (plane, plane - 1, depth, plane)]

    return pl.pallas_call(
        functools.partial(reduce_kernel, plane, depth, lines),
        out_shape=(
            jax.ShapeDtypeStruct((rows, rank), F32),
            jax.ShapeDtypeStruct((rank, snaps), F32),
        ),
        in_specs=[hbm, hbm],
        out_specs=(hbm, vmem),
        scratch_shapes=[
            pltpu.VMEM((rows, snaps), F32),
            pltpu.VMEM((snaps, rank), F32),
            pltpu.VMEM((rows, rank), F32),
            pltpu.VMEM((2 * rank, rows), BF16),
            pltpu.VMEM((rows, snaps), BF16),
            pltpu.VMEM((rows, snaps), BF16),
            pltpu.VMEM((2 * rank, 2 * rank), F32),
            pltpu.VMEM((rank, snaps), F32),
            *exchange(g_piece),
            *exchange(p_piece),
            pltpu.SemaphoreType.DMA((CHUNKS + 1,)),
            pltpu.SemaphoreType.DMA((CHUNKS,)),
            pltpu.SemaphoreType.DMA((3,)),
            pltpu.SemaphoreType.DMA((3,)),
            pltpu.SemaphoreType.DMA((3,)),
            pltpu.SemaphoreType.DMA((3,)),
        ],
        compiler_params=pltpu.CompilerParams(
            collective_id=0, has_side_effects=True, vmem_limit_bytes=48 << 20
        ),
        name="reduced",
    )(*(pltpu.with_memory_space_constraint(x, pltpu.HBM) for x in (snapshots, test_matrix)))


def solution(mesh):
    wide, lines = mesh.shape["wide"], mesh.shape["narrow"]
    plane, depth = ROW * lines, wide // ROW
    return jax.shard_map(
        functools.partial(reduced, plane, depth, lines),
        mesh=mesh,
        in_specs=(P(("wide", "narrow"), None), P()),
        out_specs=(P(("wide", "narrow"), None), P()),
        check_vma=False,
    )
```

```python
import functools
import math

import jax
import jax.numpy as jnp
from jax import lax
from jax.experimental import pallas as pl
from jax.experimental.pallas import tpu as pltpu
from jax.sharding import PartitionSpec as P

MESH = pl.DeviceIdType.MESH
ROW = 4
SHARES = (1, 2, 3, 4, 6)
PANEL = 8
TURNS = (0, 0)
F32 = jnp.float32
BF16 = jnp.bfloat16


def halves(x):
    high = x.astype(BF16)
    return high, (x - high.astype(F32)).astype(BF16)


def dot(a, b, dims=((1,), (0,))):
    return lax.dot_general(a, b, (dims, ((), ())), preferred_element_type=F32)


def flips(index, size):
    steps, unit = [0], 1
    while unit < size:
        step = (1 - 2 * lax.rem(index // unit, 2)) * unit
        steps += [step + s for s in steps]
        unit *= 2
    return steps


def inverse_factor(g):
    n = g.shape[0]
    row = lax.broadcasted_iota(jnp.int32, (n, n), 0)
    col = lax.broadcasted_iota(jnp.int32, (n, n), 1)
    w = jnp.where(row == col, F32(1), F32(0))
    at = lax.broadcasted_iota(jnp.int32, (PANEL, n), 0)
    for first in range(0, n, PANEL):
        columns = [jnp.broadcast_to(g[:, first + k:first + k + 1], g.shape) for k in range(PANEL)]
        top = [c[:PANEL] for c in columns]
        rest = [c[PANEL:] for c in columns]
        g_top, w_top = g[:PANEL], w[:PANEL]
        steps = []
        panel = jnp.zeros((PANEL, n), F32)
        for i in range(PANEL):
            r = lax.rsqrt(top[i][i:i + 1])
            u, v = g_top[i:i + 1] * r, w_top[i:i + 1] * r
            m = top[i] * r
            ahead = {}
            for k in range(i + 1, PANEL):
                ahead[k] = top[k][i:i + 1] * r
                top[k] = top[k] - m * ahead[k]
            if i + 1 < PANEL:
                g_top, w_top = g_top - m * u, w_top - m * v
            panel = jnp.where(at == i, v, panel)
            steps.append((r, u, v, ahead))
        if first + PANEL < n:
            g, w = g[PANEL:], w[PANEL:]
            for i, (r, u, v, ahead) in enumerate(steps):
                m = rest[i] * r
                for k in ahead:
                    rest[k] = rest[k] - m * ahead[k]
                g, w = g - m * u, w - m * v
        yield panel


class Exchange:
    def __init__(self, place, mine, into, slots, whole, send_sem, recv_sem):
        self.me, self.z, self.in_plane, self.along_z = place
        self.mine, self.into, self.slots, self.whole = mine, into, slots, whole
        self.send_sem, self.recv_sem = send_sem, recv_sem

    def send(self, src, dst, where, phase):
        pltpu.make_async_remote_copy(
            src_ref=src, dst_ref=dst, send_sem=self.send_sem.at[phase], recv_sem=self.recv_sem.at[phase],
            device_id=where, device_id_type=MESH,
        ).start()

    def settle(self, ref, sem):
        pltpu.make_async_copy(ref, ref, sem).wait()

    def scatter(self):
        for d, (t, where) in enumerate(self.in_plane):
            self.send(self.mine.at[t], self.into.at[d], where, 0)

    def across(self):
        self.settle(self.into, self.recv_sem.at[0])
        self.slots[self.z] = self.mine[self.me] + jnp.sum(self.into[...], axis=0)
        for where in self.along_z:
            self.send(self.slots.at[self.z], self.slots.at[self.z], where, 1)

    def gather(self):
        self.settle(self.slots.at[pl.ds(0, len(self.along_z))], self.recv_sem.at[1])
        self.whole[self.me] = jnp.sum(self.slots[...], axis=0)
        for _, where in self.in_plane:
            self.send(self.whole.at[self.me], self.whole.at[self.me], where, 2)

    def arrived(self):
        self.settle(self.into, self.recv_sem.at[2])

    def sent(self):
        self.settle(self.into, self.send_sem.at[0])
        self.settle(self.slots.at[pl.ds(0, len(self.along_z))], self.send_sem.at[1])
        self.settle(self.into, self.send_sem.at[2])


def reduce_kernel(
    plane, depth, lines,
    a_hbm, omega_hbm, basis_ref, inverse_ref, proj_ref,
    a, omega, s, sl, xt, ah, al, g_full,
    g_mine, g_in, g_z, g_all, p_mine, p_in, p_z, p_all,
    load_sem, g_send, g_recv, p_send, p_recv,
):
    rank, snaps = omega.shape[1], a.shape[1]
    unit = a.shape[0] // sum(SHARES)
    ends = [unit * sum(SHARES[:i + 1]) for i in range(len(SHARES))]
    chunks = [pl.ds(e - unit * n, unit * n) for e, n in zip(ends, SHARES)]

    load_omega = pltpu.make_async_copy(omega_hbm, omega, load_sem.at[len(chunks)])
    loads = [pltpu.make_async_copy(a_hbm.at[c], a.at[c], load_sem.at[i]) for i, c in enumerate(chunks)]
    for copy in [load_omega] + loads:
        copy.start()

    wide, narrow = lax.axis_index("wide"), lax.axis_index("narrow")
    z, me = wide // ROW, lax.rem(wide, ROW) * lines + narrow
    by_line = flips(narrow, lines)
    by_row = flips(lax.rem(wide, ROW), ROW)
    by_z = flips(z, depth)
    in_plane = [
        (me + r * lines + n, (wide + r, narrow + n)) for r in by_row for n in by_line
    ][1:]
    along_z = [(wide + d * ROW, narrow) for d in by_z][1:]

    barrier = pltpu.get_barrier_semaphore()
    for where in [w for _, w in in_plane] + along_z:
        pl.semaphore_signal(barrier, inc=1, device_id=where, device_id_type=MESH)

    place = me, z, in_plane, along_z
    gram = Exchange(place, g_mine, g_in, g_z, g_all, g_send, g_recv)
    parts = [
        Exchange(place, *(r.at[h] for r in (p_mine, p_in, p_z, p_all, p_send, p_recv))) for h in range(p_mine.shape[0])
    ]

    load_omega.wait()
    oh, ol = halves(omega[...])
    both = jnp.concatenate([oh, ol], axis=1)

    def gram_of(c):
        x_high, x_low = halves(s[c, :])
        x_t = x_high.T
        xt[:rank, c] = x_t
        sl[c, :] = x_low
        return dot(x_t, jnp.concatenate([x_high, x_low], axis=1))

    total = None
    for i in range(len(chunks) + 1):
        if i < len(chunks):
            c = chunks[i]
            loads[i].wait()
            high, low = halves(a[c, :])
            ah[c, :] = high
            al[c, :] = low
            w = dot(high, both)
            s[c, :] = w[:, :rank] + w[:, rank:] + dot(low, oh)
        if i > 0:
            term = gram_of(chunks[i - 1])
            total = term if total is None else total + term
    cross = total[:, rank:]
    g_full[...] = total[:, :rank] + cross + cross.T
    for t in range(plane):
        g_mine[t] = g_full[t * (rank // plane):(t + 1) * (rank // plane), :]
    pl.semaphore_wait(barrier, plane + depth - 2)
    gram.scatter()

    xt[rank:, :] = sl[...].T
    span = snaps // len(parts)
    tall = p_mine.shape[2]
    per = rank // tall
    for h, part in enumerate(parts):
        columns = slice(h * span, (h + 1) * span)
        w = dot(xt[...], ah[:, columns])
        proj = w[:rank] + w[rank:] + dot(xt[:rank, :], al[:, columns])
        for b in range(span // 128):
            part.mine[b * per:(b + 1) * per] = proj[:, b * 128:(b + 1) * 128].reshape(per, tall, 128)
        part.scatter()
    gram.across()
    for part in parts:
        part.across()
    gram.gather()
    for h, part in enumerate(parts):
        if TURNS[h] == 0:
            part.gather()
    gram.arrived()
    for t in range(plane):
        g_full[t * (rank // plane):(t + 1) * (rank // plane), :] = g_all[t]

    for i, panel in enumerate(inverse_factor(g_full[...])):
        inverse_ref[i * PANEL:(i + 1) * PANEL, :] = panel
        for h, part in enumerate(parts):
            if TURNS[h] == i + 1:
                part.gather()
    inverse = inverse_ref[...]
    wh, wl = halves(inverse * math.sqrt(a.shape[0] * plane * depth))
    both_w = jnp.concatenate([jnp.concatenate([wh, wh], axis=1), jnp.concatenate([wl, wl], axis=1)], axis=0)
    for c in chunks:
        x = jnp.concatenate(halves(s[c, :]), axis=1)
        w = dot(x, both_w, ((1,), (1,)))
        basis_ref[c, :] = w[:, :rank] + w[:, rank:]

    gram.sent()
    for h, part in enumerate(parts):
        part.arrived()
        for b in range(span // 128):
            proj_ref[:, h * span + b * 128:h * span + (b + 1) * 128] = (
                part.whole[b * per:(b + 1) * per].reshape(rank, 128)
            )
        part.sent()


def finish_kernel(rows, basis, inverse_ref, proj_ref, basis_hbm, coef_hbm, coef, sem):
    save = pltpu.make_async_copy(basis, basis_hbm, sem.at[0])
    save.start()
    high, low = halves(inverse_ref[...] * (1.0 / math.sqrt(rows)))
    left = jnp.concatenate([high, low, high, low], axis=1)
    for b in range(0, proj_ref.shape[1], 128):
        ph, p_low = halves(proj_ref[:, b:b + 128])
        coef[:, b:b + 128] = dot(left, jnp.concatenate([ph, ph, p_low, p_low], axis=0))
    save_coef = pltpu.make_async_copy(coef, coef_hbm, sem.at[1])
    save_coef.start()
    save_coef.wait()
    save.wait()


def on_device(plane, depth, lines, snapshots, test_matrix):
    rows, snaps = snapshots.shape
    rank = test_matrix.shape[1]
    vmem = pl.BlockSpec(memory_space=pltpu.VMEM)
    hbm = pl.BlockSpec(memory_space=pltpu.HBM)
    parts = rank * snaps // 1024 // plane
    counts = (plane, plane - 1, depth, plane)
    basis, inverse, proj = pl.pallas_call(
        functools.partial(reduce_kernel, plane, depth, lines),
        out_shape=(
            pltpu.VMEM((rows, rank), F32),
            pltpu.VMEM((rank, rank), F32),
            pltpu.VMEM((rank, snaps), F32),
        ),
        in_specs=[hbm, hbm],
        out_specs=(vmem, vmem, vmem),
        scratch_shapes=[
            pltpu.VMEM((rows, snaps), F32),
            pltpu.VMEM((snaps, rank), F32),
            pltpu.VMEM((rows, rank), F32),
            pltpu.VMEM((rows, rank), BF16),
            pltpu.VMEM((2 * rank, rows), BF16),
            pltpu.VMEM((rows, snaps), BF16),
            pltpu.VMEM((rows, snaps), BF16),
            pltpu.VMEM((rank, rank), F32),
            *[pltpu.VMEM((n, rank // plane, rank), F32) for n in counts],
            *[pltpu.VMEM((parts, n, 8, 128), F32) for n in counts],
            pltpu.SemaphoreType.DMA((len(SHARES) + 1,)),
            pltpu.SemaphoreType.DMA((3,)),
            pltpu.SemaphoreType.DMA((3,)),
            pltpu.SemaphoreType.DMA((parts, 3)),
            pltpu.SemaphoreType.DMA((parts, 3)),
        ],
        compiler_params=pltpu.CompilerParams(
            collective_id=0, has_side_effects=True, vmem_limit_bytes=44 << 20
        ),
        name="reduced",
    )(*(pltpu.with_memory_space_constraint(x, pltpu.HBM) for x in (snapshots, test_matrix)))
    return pl.pallas_call(
        functools.partial(finish_kernel, rows * plane * depth),
        out_shape=(pltpu.HBM((rows, rank), F32), pltpu.HBM((rank, snaps), F32)),
        in_specs=[vmem, vmem, vmem],
        out_specs=(hbm, hbm),
        scratch_shapes=[pltpu.VMEM((rank, snaps), F32), pltpu.SemaphoreType.DMA((2,))],
        compiler_params=pltpu.CompilerParams(vmem_limit_bytes=16 << 20),
        name="finish",
    )(basis, inverse, proj)


def solution(mesh):
    wide, lines = mesh.shape["wide"], mesh.shape["narrow"]
    plane, depth = ROW * lines, wide // ROW
    return jax.shard_map(
        functools.partial(on_device, plane, depth, lines),
        mesh=mesh,
        in_specs=(P(("wide", "narrow"), None), P()),
        out_specs=(P(("wide", "narrow"), None), P()),
        check_vma=False,
    )
```

```python
import functools
import math

import jax
import jax.numpy as jnp
from jax import lax
from jax.experimental import pallas as pl
from jax.experimental.pallas import tpu as pltpu
from jax.sharding import PartitionSpec as P

MESH = pl.DeviceIdType.MESH
ROW = 4
SHARES = (1, 2, 3, 4, 6)
PANEL = 8
EARLY = 4
PIECES = 3
F32 = jnp.float32
BF16 = jnp.bfloat16


def halves(x):
    high = x.astype(BF16)
    return high, (x - high.astype(F32)).astype(BF16)


def dot(a, b, dims=((1,), (0,))):
    return lax.dot_general(a, b, (dims, ((), ())), preferred_element_type=F32)


def flips(index, size):
    steps, unit = [0], 1
    while unit < size:
        step = (1 - 2 * lax.rem(index // unit, 2)) * unit
        steps += [step + s for s in steps]
        unit *= 2
    return steps


def inverse_factor(g):
    n, size = g.shape[0], PANEL
    shape = (size, n)
    h = g.reshape(n // size, size, n)
    lane = lax.broadcasted_iota(jnp.int32, shape, 1)
    at = lax.broadcasted_iota(jnp.int32, shape, 0)

    def row(x, i):
        return jnp.broadcast_to(x[i:i + 1], shape)

    def columns(x, first):
        return [jnp.broadcast_to(x[..., first + k:first + k + 1], x.shape) for k in range(size)]

    block = columns(h[0], 0)
    for first in range(0, n, size):
        last = first + size == n
        if not last:
            rest = columns(h[1:], first)
            later = columns(h[1], first + size)
        u = {(i, k): row(block[k], i) for i in range(size) for k in range(i, size)}
        here = (lane >= first) & (lane < first + size)
        top = jnp.where(here, jnp.where(lane == at + first, F32(1), F32(0)), h[0])
        rows = [row(top, i) for i in range(size)]
        scale = []
        for i in range(size):
            r = lax.rsqrt(u[i, i])
            scale.append(r)
            for k in range(i + 1, size):
                u[i, k] = u[i, k] * r
            for k in range(i + 1, size):
                for m in range(k, size):
                    u[k, m] = u[k, m] - u[i, k] * u[i, m]
            rows[i] = rows[i] * r
            for k in range(i + 1, size):
                rows[k] = rows[k] - u[i, k] * rows[i]
        panel = rows[0]
        for i in range(1, size):
            panel = jnp.where(at == i, rows[i], panel)
        yield jnp.where(lane < first + size, panel, F32(0))
        if not last:
            h = jnp.where(here[None], F32(0), h[1:])
            for i in range(size):
                factor = rest[i] * scale[i][None]
                near = factor[0]
                for k in range(size):
                    later[k] = later[k] - near * near[k:k + 1]
                for k in range(i + 1, size):
                    rest[k] = rest[k] - factor * u[i, k][None]
                h = h - factor * rows[i][None]
            block = later


def basis_of(rows, weights):
    rank = rows.shape[1]
    w = dot(jnp.concatenate(halves(rows), axis=1), weights, ((1,), (1,)))
    return w[:, :rank] + w[:, rank:]


class Exchange:
    def __init__(self, place, mine, into, slots, whole, send_sem, recv_sem):
        self.me, self.z, self.in_plane, self.along_z = place
        self.mine, self.into, self.slots, self.whole = mine, into, slots, whole
        self.send_sem, self.recv_sem = send_sem, recv_sem

    def send(self, src, dst, where, phase):
        pltpu.make_async_remote_copy(
            src_ref=src, dst_ref=dst, send_sem=self.send_sem.at[phase], recv_sem=self.recv_sem.at[phase],
            device_id=where, device_id_type=MESH,
        ).start()

    def settle(self, ref, sem):
        pltpu.make_async_copy(ref, ref, sem).wait()

    def scatter(self):
        for d, (t, where) in enumerate(self.in_plane):
            self.send(self.mine.at[t], self.into.at[d], where, 0)

    def across(self):
        self.settle(self.into, self.recv_sem.at[0])
        self.slots[self.z] = self.mine[self.me] + jnp.sum(self.into[...], axis=0)
        for where in self.along_z:
            self.send(self.slots.at[self.z], self.slots.at[self.z], where, 1)

    def gather(self):
        self.settle(self.slots.at[pl.ds(0, len(self.along_z))], self.recv_sem.at[1])
        self.whole[self.me] = jnp.sum(self.slots[...], axis=0)
        for _, where in self.in_plane:
            self.send(self.whole.at[self.me], self.whole.at[self.me], where, 2)

    def arrived(self):
        self.settle(self.into, self.recv_sem.at[2])

    def sent(self):
        self.settle(self.into, self.send_sem.at[0])
        self.settle(self.slots.at[pl.ds(0, len(self.along_z))], self.send_sem.at[1])
        self.settle(self.into, self.send_sem.at[2])


def reduce_kernel(
    plane, depth, lines,
    a_hbm, omega_hbm, s, first_ref, weights_ref, left_ref, proj_ref,
    a, omega, inverse_ref, sl, xt, ah, al, g_full,
    g_mine, g_in, g_z, g_all, p_mine, p_in, p_z, p_all,
    load_sem, g_send, g_recv, p_send, p_recv,
):
    rank, snaps = omega.shape[1], a.shape[1]
    unit = a.shape[0] // sum(SHARES)
    ends = [unit * sum(SHARES[:i + 1]) for i in range(len(SHARES))]
    chunks = [pl.ds(e - unit * n, unit * n) for e, n in zip(ends, SHARES)]

    load_omega = pltpu.make_async_copy(omega_hbm, omega, load_sem.at[len(chunks)])
    loads = [pltpu.make_async_copy(a_hbm.at[c], a.at[c], load_sem.at[i]) for i, c in enumerate(chunks)]
    for copy in [load_omega] + loads:
        copy.start()

    wide, narrow = lax.axis_index("wide"), lax.axis_index("narrow")
    z, me = wide // ROW, lax.rem(wide, ROW) * lines + narrow
    by_line = flips(narrow, lines)
    by_row = flips(lax.rem(wide, ROW), ROW)
    by_z = flips(z, depth)
    in_plane = [
        (me + r * lines + n, (wide + r, narrow + n)) for r in by_row for n in by_line
    ][1:]
    along_z = [(wide + d * ROW, narrow) for d in by_z][1:]

    barrier = pltpu.get_barrier_semaphore()
    for where in [w for _, w in in_plane] + along_z:
        pl.semaphore_signal(barrier, inc=1, device_id=where, device_id_type=MESH)

    place = me, z, in_plane, along_z
    gram = Exchange(place, g_mine, g_in, g_z, g_all, g_send, g_recv)
    parts = [
        Exchange(place, *(r.at[h] for r in (p_mine, p_in, p_z, p_all, p_send, p_recv))) for h in range(p_mine.shape[0])
    ]

    load_omega.wait()
    oh, ol = halves(omega[...])
    both = jnp.concatenate([oh, ol], axis=1)

    def gram_of(c):
        x_high, x_low = halves(s[c, :])
        x_t = x_high.T
        xt[:rank, c] = x_t
        sl[c, :] = x_low
        return dot(x_t, jnp.concatenate([x_high, x_low], axis=1))

    total = None
    for i in range(len(chunks) + 1):
        if i < len(chunks):
            c = chunks[i]
            loads[i].wait()
            high, low = halves(a[c, :])
            ah[c, :] = high
            al[c, :] = low
            w = dot(high, both)
            s[c, :] = w[:, :rank] + w[:, rank:] + dot(low, oh)
        if i > 0:
            term = gram_of(chunks[i - 1])
            total = term if total is None else total + term
    cross = total[:, rank:]
    g_full[...] = total[:, :rank] + cross + cross.T
    pieces = [slice(t * (rank // plane), (t + 1) * (rank // plane)) for t in range(plane)]
    for t, piece in enumerate(pieces):
        g_mine[t] = g_full[piece, :]
    pl.semaphore_wait(barrier, plane + depth - 2)
    gram.scatter()

    xt[rank:, :] = sl[...].T
    span = snaps // len(parts)
    for first in range(0, snaps, 2 * span):
        w = dot(xt[...], ah[:, first:first + 2 * span])
        proj_ref[:, first:first + 2 * span] = (
            w[:rank] + w[rank:] + dot(xt[:rank, :], al[:, first:first + 2 * span])
        )
        for q in (first // span, first // span + 1):
            for t, piece in enumerate(pieces):
                parts[q].mine[t] = proj_ref[piece, q * span:(q + 1) * span]
            parts[q].scatter()
    gram.across()
    for part in parts:
        part.across()
    gram.gather()
    for part in parts:
        part.gather()
    gram.arrived()
    for t, piece in enumerate(pieces):
        g_full[piece, :] = g_all[t]

    for i, panel in enumerate(inverse_factor(g_full[...])):
        inverse_ref[i * PANEL:(i + 1) * PANEL, :] = panel
    inverse, scale = inverse_ref[...], math.sqrt(a.shape[0] * plane * depth)
    wh, wl = halves(inverse * scale)
    weights_ref[...] = jnp.concatenate(
        [jnp.concatenate([wh, wh], axis=1), jnp.concatenate([wl, wl], axis=1)], axis=0
    )
    left_ref[...] = jnp.concatenate(halves(inverse * (1.0 / scale)) * 2, axis=1)
    early = first_ref.shape[0]
    first_ref[...] = basis_of(s[:early, :], weights_ref[...])

    gram.sent()
    for q, part in enumerate(parts):
        part.arrived()
        for t, piece in enumerate(pieces):
            proj_ref[piece, q * span:(q + 1) * span] = part.whole[t]
        part.sent()


def finish_kernel(s, first, weights, left, proj_ref, basis_hbm, coef_hbm, basis, coef, sem):
    rows, early = s.shape[0], first.shape[0]
    saves = [pltpu.make_async_copy(first, basis_hbm.at[pl.ds(0, early)], sem.at[0])]
    saves[0].start()
    span = (rows - early) // PIECES
    for i in range(PIECES):
        c = pl.ds(early + i * span, span)
        basis[c, :] = basis_of(s[c, :], weights[...])
        saves.append(pltpu.make_async_copy(basis.at[c], basis_hbm.at[c], sem.at[i + 1]))
        saves[-1].start()
    for b in range(0, proj_ref.shape[1], 128):
        ph, p_low = halves(proj_ref[:, b:b + 128])
        coef[:, b:b + 128] = dot(left[...], jnp.concatenate([ph, ph, p_low, p_low], axis=0))
    saves.append(pltpu.make_async_copy(coef, coef_hbm, sem.at[PIECES + 1]))
    saves[-1].start()
    for save in saves:
        save.wait()


def on_device(plane, depth, lines, snapshots, test_matrix):
    rows, snaps = snapshots.shape
    rank = test_matrix.shape[1]
    vmem = pl.BlockSpec(memory_space=pltpu.VMEM)
    hbm = pl.BlockSpec(memory_space=pltpu.HBM)
    parts = snaps // rank
    counts = (plane, plane - 1, depth, plane)
    results = pl.pallas_call(
        functools.partial(reduce_kernel, plane, depth, lines),
        out_shape=(
            pltpu.VMEM((rows, rank), F32),
            pltpu.VMEM((rows // EARLY, rank), F32),
            pltpu.VMEM((2 * rank, 2 * rank), BF16),
            pltpu.VMEM((rank, 4 * rank), BF16),
            pltpu.VMEM((rank, snaps), F32),
        ),
        in_specs=[hbm, hbm],
        out_specs=(vmem,) * 5,
        scratch_shapes=[
            pltpu.VMEM((rows, snaps), F32),
            pltpu.VMEM((snaps, rank), F32),
            pltpu.VMEM((rank, rank), F32),
            pltpu.VMEM((rows, rank), BF16),
            pltpu.VMEM((2 * rank, rows), BF16),
            pltpu.VMEM((rows, snaps), BF16),
            pltpu.VMEM((rows, snaps), BF16),
            pltpu.VMEM((rank, rank), F32),
            *[pltpu.VMEM((n, rank // plane, rank), F32) for n in counts],
            *[pltpu.VMEM((parts, n, rank // plane, rank), F32) for n in counts],
            pltpu.SemaphoreType.DMA((len(SHARES) + 1,)),
            pltpu.SemaphoreType.DMA((3,)),
            pltpu.SemaphoreType.DMA((3,)),
            pltpu.SemaphoreType.DMA((parts, 3)),
            pltpu.SemaphoreType.DMA((parts, 3)),
        ],
        compiler_params=pltpu.CompilerParams(
            collective_id=0, has_side_effects=True, vmem_limit_bytes=40 << 20
        ),
        name="reduced",
    )(*(pltpu.with_memory_space_constraint(x, pltpu.HBM) for x in (snapshots, test_matrix)))
    return pl.pallas_call(
        finish_kernel,
        out_shape=(pltpu.HBM((rows, rank), F32), pltpu.HBM((rank, snaps), F32)),
        in_specs=[vmem] * 5,
        out_specs=(hbm, hbm),
        scratch_shapes=[
            pltpu.VMEM((rows, rank), F32),
            pltpu.VMEM((rank, snaps), F32),
            pltpu.SemaphoreType.DMA((PIECES + 2,)),
        ],
        compiler_params=pltpu.CompilerParams(vmem_limit_bytes=16 << 20),
        name="finish",
    )(*results)


def solution(mesh):
    wide, lines = mesh.shape["wide"], mesh.shape["narrow"]
    plane, depth = ROW * lines, wide // ROW
    return jax.shard_map(
        functools.partial(on_device, plane, depth, lines),
        mesh=mesh,
        in_specs=(P(("wide", "narrow"), None), P()),
        out_specs=(P(("wide", "narrow"), None), P()),
        check_vma=False,
    )
```

```python
import functools
import math

import jax
import jax.numpy as jnp
from jax import lax
from jax.experimental import pallas as pl
from jax.experimental.pallas import tpu as pltpu
from jax.sharding import PartitionSpec as P

MESH = pl.DeviceIdType.MESH
ROW = 4
SHARES = (1, 2, 3, 4, 6)
PANEL = 8
EARLY = 4
PIECES = 6
F32 = jnp.float32
BF16 = jnp.bfloat16


def halves(x):
    high = x.astype(BF16)
    return high, (x - high.astype(F32)).astype(BF16)


def dot(a, b, dims=((1,), (0,))):
    return lax.dot_general(a, b, (dims, ((), ())), preferred_element_type=F32)


def flips(index, size):
    steps, unit = [0], 1
    while unit < size:
        step = (1 - 2 * lax.rem(index // unit, 2)) * unit
        steps += [step + s for s in steps]
        unit *= 2
    return steps


def inverse_factor(g):
    n, size = g.shape[0], PANEL
    shape = (size, n)
    h = g.reshape(n // size, size, n)
    lane = lax.broadcasted_iota(jnp.int32, shape, 1)
    at = lax.broadcasted_iota(jnp.int32, shape, 0)

    def row(x, i):
        return jnp.broadcast_to(x[i:i + 1], shape)

    def columns(x, first):
        return [jnp.broadcast_to(x[..., first + k:first + k + 1], x.shape) for k in range(size)]

    block = columns(h[0], 0)
    for first in range(0, n, size):
        last = first + size == n
        if not last:
            rest = columns(h[1:], first)
            later = columns(h[1], first + size)
        u = {(i, k): row(block[k], i) for i in range(size) for k in range(i, size)}
        here = (lane >= first) & (lane < first + size)
        top = jnp.where(here, jnp.where(lane == at + first, F32(1), F32(0)), h[0])
        rows = [row(top, i) for i in range(size)]
        scale = []
        for i in range(size):
            r = lax.rsqrt(u[i, i])
            scale.append(r)
            for k in range(i + 1, size):
                u[i, k] = u[i, k] * r
            for k in range(i + 1, size):
                for m in range(k, size):
                    u[k, m] = u[k, m] - u[i, k] * u[i, m]
            rows[i] = rows[i] * r
            for k in range(i + 1, size):
                rows[k] = rows[k] - u[i, k] * rows[i]
        panel = rows[0]
        for i in range(1, size):
            panel = jnp.where(at == i, rows[i], panel)
        yield jnp.where(lane < first + size, panel, F32(0))
        if not last:
            h = jnp.where(here[None], F32(0), h[1:])
            for i in range(size):
                factor = rest[i] * scale[i][None]
                near = factor[0]
                for k in range(size):
                    later[k] = later[k] - near * near[k:k + 1]
                for k in range(i + 1, size):
                    rest[k] = rest[k] - factor * u[i, k][None]
                h = h - factor * rows[i][None]
            block = later


def basis_of(rows, weights):
    rank = rows.shape[1]
    w = dot(jnp.concatenate(halves(rows), axis=1), weights, ((1,), (1,)))
    return w[:, :rank] + w[:, rank:]


class Exchange:
    def __init__(self, place, mine, into, slots, whole, send_sem, recv_sem):
        self.me, self.z, self.in_plane, self.along_z = place
        self.mine, self.into, self.slots, self.whole = mine, into, slots, whole
        self.send_sem, self.recv_sem = send_sem, recv_sem

    def send(self, src, dst, where, phase):
        pltpu.make_async_remote_copy(
            src_ref=src, dst_ref=dst, send_sem=self.send_sem.at[phase], recv_sem=self.recv_sem.at[phase],
            device_id=where, device_id_type=MESH,
        ).start()

    def settle(self, ref, sem):
        pltpu.make_async_copy(ref, ref, sem).wait()

    def scatter(self):
        for d, (t, where) in enumerate(self.in_plane):
            self.send(self.mine.at[t], self.into.at[d], where, 0)

    def across(self):
        self.settle(self.into, self.recv_sem.at[0])
        self.slots[self.z] = self.mine[self.me] + jnp.sum(self.into[...], axis=0)
        for where in self.along_z:
            self.send(self.slots.at[self.z], self.slots.at[self.z], where, 1)

    def gather(self):
        self.settle(self.slots.at[pl.ds(0, len(self.along_z))], self.recv_sem.at[1])
        self.whole[self.me] = jnp.sum(self.slots[...], axis=0)
        for _, where in self.in_plane:
            self.send(self.whole.at[self.me], self.whole.at[self.me], where, 2)

    def arrived(self):
        self.settle(self.into, self.recv_sem.at[2])

    def sent(self):
        self.settle(self.into, self.send_sem.at[0])
        self.settle(self.slots.at[pl.ds(0, len(self.along_z))], self.send_sem.at[1])
        self.settle(self.into, self.send_sem.at[2])


def reduce_kernel(
    plane, depth, lines,
    a_hbm, omega_hbm, s, first_ref, weights_ref, left_ref, proj_ref,
    a, omega, inverse_ref, sl, xt, ah, al, g_full,
    g_mine, g_in, g_z, g_all, p_mine, p_in, p_z, p_all,
    load_sem, g_send, g_recv, p_send, p_recv,
):
    rank, snaps = omega.shape[1], a.shape[1]
    unit = a.shape[0] // sum(SHARES)
    ends = [unit * sum(SHARES[:i + 1]) for i in range(len(SHARES))]
    chunks = [pl.ds(e - unit * n, unit * n) for e, n in zip(ends, SHARES)]

    load_omega = pltpu.make_async_copy(omega_hbm, omega, load_sem.at[len(chunks)])
    loads = [pltpu.make_async_copy(a_hbm.at[c], a.at[c], load_sem.at[i]) for i, c in enumerate(chunks)]
    for copy in [load_omega] + loads:
        copy.start()

    wide, narrow = lax.axis_index("wide"), lax.axis_index("narrow")
    z, me = wide // ROW, lax.rem(wide, ROW) * lines + narrow
    by_line = flips(narrow, lines)
    by_row = flips(lax.rem(wide, ROW), ROW)
    by_z = flips(z, depth)
    in_plane = [
        (me + r * lines + n, (wide + r, narrow + n)) for r in by_row for n in by_line
    ][1:]
    along_z = [(wide + d * ROW, narrow) for d in by_z][1:]

    barrier = pltpu.get_barrier_semaphore()
    for where in [w for _, w in in_plane] + along_z:
        pl.semaphore_signal(barrier, inc=1, device_id=where, device_id_type=MESH)

    place = me, z, in_plane, along_z
    gram = Exchange(place, g_mine, g_in, g_z, g_all, g_send, g_recv)
    parts = [
        Exchange(place, *(r.at[h] for r in (p_mine, p_in, p_z, p_all, p_send, p_recv))) for h in range(p_mine.shape[0])
    ]

    load_omega.wait()
    oh, ol = halves(omega[...])
    both = jnp.concatenate([oh, ol], axis=1)

    def gram_of(c):
        x_high, x_low = halves(s[c, :])
        x_t = x_high.T
        xt[:rank, c] = x_t
        sl[c, :] = x_low
        return dot(x_t, jnp.concatenate([x_high, x_low], axis=1))

    total = None
    for i in range(len(chunks) + 1):
        if i < len(chunks):
            c = chunks[i]
            loads[i].wait()
            high, low = halves(a[c, :])
            ah[c, :] = high
            al[c, :] = low
            w = dot(high, both)
            s[c, :] = w[:, :rank] + w[:, rank:] + dot(low, oh)
        if i > 0:
            term = gram_of(chunks[i - 1])
            total = term if total is None else total + term
    cross = total[:, rank:]
    g_full[...] = total[:, :rank] + cross + cross.T
    pieces = [slice(t * (rank // plane), (t + 1) * (rank // plane)) for t in range(plane)]
    for t, piece in enumerate(pieces):
        g_mine[t] = g_full[piece, :]
    pl.semaphore_wait(barrier, plane + depth - 2)
    gram.scatter()

    xt[rank:, :] = sl[...].T
    span = snaps // len(parts)
    for first in range(0, snaps, 2 * span):
        w = dot(xt[...], ah[:, first:first + 2 * span])
        proj_ref[:, first:first + 2 * span] = (
            w[:rank] + w[rank:] + dot(xt[:rank, :], al[:, first:first + 2 * span])
        )
        for q in (first // span, first // span + 1):
            for t, piece in enumerate(pieces):
                parts[q].mine[t] = proj_ref[piece, q * span:(q + 1) * span]
            parts[q].scatter()
    gram.across()
    for part in parts:
        part.across()
    gram.gather()
    for part in parts:
        part.gather()
    gram.arrived()
    for t, piece in enumerate(pieces):
        g_full[piece, :] = g_all[t]

    for i, panel in enumerate(inverse_factor(g_full[...])):
        inverse_ref[i * PANEL:(i + 1) * PANEL, :] = panel
    inverse, scale = inverse_ref[...], math.sqrt(a.shape[0] * plane * depth)
    wh, wl = halves(inverse * scale)
    weights_ref[...] = jnp.concatenate(
        [jnp.concatenate([wh, wh], axis=1), jnp.concatenate([wl, wl], axis=1)], axis=0
    )
    left_ref[...] = jnp.concatenate(halves(inverse * (1.0 / scale)) * 2, axis=1)
    early = first_ref.shape[0]
    first_ref[...] = basis_of(s[:early, :], weights_ref[...])

    gram.sent()
    for q, part in enumerate(parts):
        part.arrived()
        for t, piece in enumerate(pieces):
            proj_ref[piece, q * span:(q + 1) * span] = part.whole[t]
        part.sent()


def finish_kernel(s, first, weights, left, proj_ref, basis_hbm, coef_hbm, basis, coef, sem):
    rows, early = s.shape[0], first.shape[0]
    saves = [pltpu.make_async_copy(first, basis_hbm.at[pl.ds(0, early)], sem.at[0])]
    saves[0].start()
    span = (rows - early) // PIECES
    for i in range(PIECES):
        c = pl.ds(early + i * span, span)
        basis[c, :] = basis_of(s[c, :], weights[...])
        saves.append(pltpu.make_async_copy(basis.at[c], basis_hbm.at[c], sem.at[i + 1]))
        saves[-1].start()
    for b in range(0, proj_ref.shape[1], 128):
        ph, p_low = halves(proj_ref[:, b:b + 128])
        coef[:, b:b + 128] = dot(left[...], jnp.concatenate([ph, ph, p_low, p_low], axis=0))
    saves.append(pltpu.make_async_copy(coef, coef_hbm, sem.at[PIECES + 1]))
    saves[-1].start()
    for save in saves:
        save.wait()


def on_device(plane, depth, lines, snapshots, test_matrix):
    rows, snaps = snapshots.shape
    rank = test_matrix.shape[1]
    vmem = pl.BlockSpec(memory_space=pltpu.VMEM)
    hbm = pl.BlockSpec(memory_space=pltpu.HBM)
    parts = snaps // rank
    counts = (plane, plane - 1, depth, plane)
    results = pl.pallas_call(
        functools.partial(reduce_kernel, plane, depth, lines),
        out_shape=(
            pltpu.VMEM((rows, rank), F32),
            pltpu.VMEM((rows // EARLY, rank), F32),
            pltpu.VMEM((2 * rank, 2 * rank), BF16),
            pltpu.VMEM((rank, 4 * rank), BF16),
            pltpu.VMEM((rank, snaps), F32),
        ),
        in_specs=[hbm, hbm],
        out_specs=(vmem,) * 5,
        scratch_shapes=[
            pltpu.VMEM((rows, snaps), F32),
            pltpu.VMEM((snaps, rank), F32),
            pltpu.VMEM((rank, rank), F32),
            pltpu.VMEM((rows, rank), BF16),
            pltpu.VMEM((2 * rank, rows), BF16),
            pltpu.VMEM((rows, snaps), BF16),
            pltpu.VMEM((rows, snaps), BF16),
            pltpu.VMEM((rank, rank), F32),
            *[pltpu.VMEM((n, rank // plane, rank), F32) for n in counts],
            *[pltpu.VMEM((parts, n, rank // plane, rank), F32) for n in counts],
            pltpu.SemaphoreType.DMA((len(SHARES) + 1,)),
            pltpu.SemaphoreType.DMA((3,)),
            pltpu.SemaphoreType.DMA((3,)),
            pltpu.SemaphoreType.DMA((parts, 3)),
            pltpu.SemaphoreType.DMA((parts, 3)),
        ],
        compiler_params=pltpu.CompilerParams(
            collective_id=0, has_side_effects=True, vmem_limit_bytes=40 << 20
        ),
        name="reduced",
    )(*(pltpu.with_memory_space_constraint(x, pltpu.HBM) for x in (snapshots, test_matrix)))
    return pl.pallas_call(
        finish_kernel,
        out_shape=(pltpu.HBM((rows, rank), F32), pltpu.HBM((rank, snaps), F32)),
        in_specs=[vmem] * 5,
        out_specs=(hbm, hbm),
        scratch_shapes=[
            pltpu.VMEM((rows, rank), F32),
            pltpu.VMEM((rank, snaps), F32),
            pltpu.SemaphoreType.DMA((PIECES + 2,)),
        ],
        compiler_params=pltpu.CompilerParams(vmem_limit_bytes=16 << 20),
        name="finish",
    )(*results)


def solution(mesh):
    wide, lines = mesh.shape["wide"], mesh.shape["narrow"]
    plane, depth = ROW * lines, wide // ROW
    return jax.shard_map(
        functools.partial(on_device, plane, depth, lines),
        mesh=mesh,
        in_specs=(P(("wide", "narrow"), None), P()),
        out_specs=(P(("wide", "narrow"), None), P()),
        check_vma=False,
    )
```
